256 devices in a mesh: ctx: 64 (over y, z_lo, x), enc: 4 (over z_hi, core).
Axes of the slice: x: 4, y: 4, z: 8 (z_hi: 2, z_lo: 4; z = z_hi * 4 + z_lo), core: 2. Of those that a mesh axis runs over, the one named last changes fastest.
Arguments:
- qkv: bfloat16 [3, 32768, 4096], P(None, ('ctx', 'enc')), may hold values from -12 to 12
- grad_out: bfloat16 [32768, 4096], P(('ctx', 'enc')), may hold values from -6 to 6
- text_kv: bfloat16 [2, 256, 4096], P(None, 'ctx', 'enc'), may hold values from -12 to 12
- text_len: int32 [1], replicated, may hold values from 128 to 256
- key_tiles: int32 [64, 3], replicated, may hold values from 0 to 63, as said below
- key_count: int32 [64], replicated, may hold values from 2 to 3, as said below
Outputs:
- attn_out: bfloat16 [32768, 4096], P(('ctx', 'enc'))
- grad_q: float32 [32768, 4096], P(('ctx', 'enc'))
- grad_k: float32 [32768, 4096], P(('ctx', 'enc'))
- grad_v: float32 [32768, 4096], P(('ctx', 'enc'))
- grad_text: float32 [2, 256, 4096], P(None, 'ctx', 'enc')
The draws below stay inside these ranges and needn't reach their ends.
Inputs may be any that keep to these rules, and one draw needn't show every extreme that they name: `key_tiles`: row i lists key tiles of query tile i: its first entry is i, its entries are distinct and within 2 tiles of i. Only the first key_count[i] entries are used; the others are further such tiles. `key_count`: some query tile uses all 3 entries in every draw.
All inputs are finite; a program needn't handle non-finite values.
Results may differ from the reference program's by a relative error of at most 0.012.
Values may be sent and summed in bfloat16 or wider, within the bound.
No kernel may reach another device: no remote copies, remote signals or barrier semaphores. Data moves between devices by JAX's collectives and lax.ppermute only.
A program may use at most 192 MiB of HBM per device.

```python
import jax
import jax.numpy as jnp
from jax import lax

TOK_DEV = 512
HEADS = 32
HD = 128
TEXT = 256
REACH = 2
SLOTS = 3
TILES = 64
TOKENS = 32768
FEATS = 4096


def draw_qkv(key, part):
    parts = jax.random.split(jax.random.fold_in(key, 11), 3)
    shape = (TOKENS, FEATS)
    queries = jnp.clip(1.5 * jax.random.normal(parts[0], shape, jnp.float32), -6.0, 6.0)
    keys_raw = jnp.clip(jax.random.normal(parts[1], shape, jnp.float32), -4.0, 4.0)
    values = jnp.clip(3.0 * jax.random.normal(parts[2], shape, jnp.float32), -12.0, 12.0)
    return jnp.stack([queries, keys_raw, values]).astype(jnp.bfloat16)


def draw_text_kv(key, part):
    parts = jax.random.split(jax.random.fold_in(key, 13), 2)
    shape = (TEXT, FEATS)
    keys_raw = jnp.clip(jax.random.normal(parts[0], shape, jnp.float32), -4.0, 4.0)
    values = jnp.clip(3.0 * jax.random.normal(parts[1], shape, jnp.float32), -12.0, 12.0)
    return jnp.stack([keys_raw, values]).astype(jnp.bfloat16)


def draw_key_tiles(key, part):
    inner = jax.random.fold_in(key, 31)
    tile = jnp.arange(TILES, dtype=jnp.int32)[:, None]
    offsets = jnp.array([step for step in range(-REACH, REACH + 1) if step != 0], dtype=jnp.int32)
    target = tile + offsets[None, :]
    valid = (target >= 0) & (target < TILES)
    ranking = jax.random.randint(inner, (TILES, 2 * REACH), 0, 4096) * 16
    ranking = ranking + jnp.arange(2 * REACH, dtype=jnp.int32)[None, :] + jnp.where(valid, 0, 1 << 20)
    order = jnp.argsort(ranking, axis=1, stable=True)
    picked = jnp.take_along_axis(target, order, axis=1)[:, :SLOTS - 1]
    return jnp.concatenate([tile, picked], axis=1).astype(jnp.int32)


def draw_key_count(key, part):
    parts = jax.random.split(jax.random.fold_in(key, 41), 3)
    base = 2 + (jax.random.randint(parts[0], (TILES,), 0, 3) == 0).astype(jnp.int32)
    heavy = jax.random.randint(parts[1], (TILES,), 0, 8) == 0
    forced = jnp.arange(TILES) == jax.random.randint(parts[2], (), 0, TILES)
    return jnp.minimum(jnp.where(heavy | forced, SLOTS, base), SLOTS).astype(jnp.int32)


def block_scale(stream_key, extent, cuts, least, high):
    factor_of, own = 1.0, jax.random.fold_in(stream_key, 6)
    for axis_at, shards_of in cuts:
        steps = jnp.exp(jax.random.uniform(jax.random.fold_in(own, axis_at), (shards_of,), jnp.float32, least / len(cuts), high / len(cuts)))
        factor_of = factor_of * jnp.repeat(steps, extent[axis_at] // shards_of).reshape([-1 if axis == axis_at else 1 for axis in range(len(extent))])
    return factor_of


def scatter_about(own_key, dims, deviation, limit, cuts=(), kind=jnp.bfloat16):
    result = jax.random.normal(own_key, dims, jnp.float32) * deviation
    if len(cuts) > 0:
        result = block_scale(own_key, dims, cuts, -0.22, 0.18) * result
    return jnp.clip(result, min=-limit, max=limit).astype(kind)


def setup_inputs(seed: int = 0) -> dict:
    key_of = jax.random.split(jax.random.key(seed), 7)
    qkv = draw_qkv(jax.random.fold_in(key_of[6], 71), 0)
    grad_out = scatter_about(key_of[1], (TOKENS, FEATS), 1.0, 6.0, ((0, 256),))
    text_kv = draw_text_kv(jax.random.fold_in(key_of[6], 71), 0)
    text_len = jax.random.randint(key_of[3], (1,), TEXT // 2, TEXT + 1).astype(jnp.int32)
    key_tiles = draw_key_tiles(jax.random.fold_in(key_of[6], 71), 0)
    key_count = draw_key_count(jax.random.fold_in(key_of[6], 71), 0)
    return {"qkv": qkv, "grad_out": grad_out, "text_kv": text_kv, "text_len": text_len, "key_tiles": key_tiles, "key_count": key_count}


MASKED_SCORE = -1e30


def log_norm_of(scores):
    row_max = jnp.max(scores, axis=-1, keepdims=True)
    return row_max + jnp.log(jnp.sum(jnp.exp(scores - row_max), axis=-1, keepdims=True))


def rounded(values):
    return lax.optimization_barrier(values.astype(jnp.bfloat16)).astype(jnp.float32)


def tile_rows(array, tile):
    start = (tile * TOK_DEV).astype(jnp.int32)
    return lax.dynamic_slice_in_dim(array, start, TOK_DEV, 0)


def reference(qkv, grad_out, text_kv, text_len, key_tiles, key_count):
    inv_root = HD ** -0.5
    text_keys = text_kv[0].astype(jnp.float32).reshape(TEXT, HEADS, HD)
    text_values = text_kv[1].astype(jnp.float32).reshape(TEXT, HEADS, HD)
    text_live = jnp.arange(TEXT) < text_len[0]
    slot_ids = jnp.arange(SLOTS)

    def one_tile(carry, tile):
        grad_key, grad_value, text_dkey, text_dvalue = carry
        queries = tile_rows(qkv[0], tile).astype(jnp.float32).reshape(TOK_DEV, HEADS, HD)
        grad_rows = tile_rows(grad_out, tile).astype(jnp.float32).reshape(TOK_DEV, HEADS, HD)
        tile_list = key_tiles[tile]
        slot_live = slot_ids < key_count[tile]
        key_rows = jnp.concatenate([tile_rows(qkv[1], tile_list[slot]) for slot in range(SLOTS)], 0)
        key_rows = key_rows.astype(jnp.float32).reshape(SLOTS * TOK_DEV, HEADS, HD)
        value_rows = jnp.concatenate([tile_rows(qkv[2], tile_list[slot]) for slot in range(SLOTS)], 0)
        value_rows = value_rows.astype(jnp.float32).reshape(SLOTS * TOK_DEV, HEADS, HD)
        key_live = jnp.repeat(slot_live, TOK_DEV)
        scores = jnp.einsum("qhd,khd->hqk", queries, key_rows) * inv_root
        scores = jnp.where(key_live[None, None, :], scores, MASKED_SCORE)
        attn_probs = rounded(jnp.exp(scores - log_norm_of(scores)))
        self_out = jnp.einsum("hqk,khd->qhd", attn_probs, value_rows)
        text_scores = jnp.einsum("qhd,khd->hqk", queries, text_keys) * inv_root
        text_scores = jnp.where(text_live[None, None, :], text_scores, MASKED_SCORE)
        text_probs = rounded(jnp.exp(text_scores - log_norm_of(text_scores)))
        text_out = jnp.einsum("hqk,khd->qhd", text_probs, text_values)
        attn_rows = (self_out + text_out).astype(jnp.bfloat16).reshape(TOK_DEV, FEATS)
        self_dot = jnp.sum(grad_rows * self_out, axis=-1).T[:, :, None]
        text_dot = jnp.sum(grad_rows * text_out, axis=-1).T[:, :, None]
        score_grads = rounded(inv_root * attn_probs * (jnp.einsum("qhd,khd->hqk", grad_rows, value_rows) - self_dot))
        text_sgrads = rounded(inv_root * text_probs * (jnp.einsum("qhd,khd->hqk", grad_rows, text_values) - text_dot))
        grad_query = jnp.einsum("hqk,khd->qhd", score_grads, key_rows) + jnp.einsum("hqk,khd->qhd", text_sgrads, text_keys)
        tile_dkey = rounded(jnp.einsum("hqk,qhd->khd", score_grads, queries).reshape(SLOTS, TOK_DEV, FEATS))
        tile_dvalue = rounded(jnp.einsum("hqk,qhd->khd", attn_probs, grad_rows).reshape(SLOTS, TOK_DEV, FEATS))
        for slot in range(SLOTS):
            start = (tile_list[slot] * TOK_DEV).astype(jnp.int32)
            grad_key = lax.dynamic_update_slice_in_dim(grad_key, lax.dynamic_slice_in_dim(grad_key, start, TOK_DEV, 0) + tile_dkey[slot], start, 0)
            grad_value = lax.dynamic_update_slice_in_dim(grad_value, lax.dynamic_slice_in_dim(grad_value, start, TOK_DEV, 0) + tile_dvalue[slot], start, 0)
        text_dkey = text_dkey + jnp.einsum("hqk,qhd->khd", text_sgrads, queries)
        text_dvalue = text_dvalue + jnp.einsum("hqk,qhd->khd", text_probs, grad_rows)
        return (grad_key, grad_value, text_dkey, text_dvalue), (attn_rows, grad_query.reshape(TOK_DEV, FEATS))

    initial = (jnp.zeros((TOKENS, FEATS), jnp.float32), jnp.zeros((TOKENS, FEATS), jnp.float32),
               jnp.zeros((TEXT, HEADS, HD), jnp.float32), jnp.zeros((TEXT, HEADS, HD), jnp.float32))
    final, stacked = lax.scan(one_tile, initial, jnp.arange(TILES, dtype=jnp.int32))
    grad_key, grad_value, text_dkey, text_dvalue = final
    attn_rows, grad_queries = stacked
    grad_text = jnp.stack([text_dkey.reshape(TEXT, FEATS), text_dvalue.reshape(TEXT, FEATS)])
    return (attn_rows.reshape(TOKENS, FEATS), grad_queries.reshape(TOKENS, FEATS), grad_key, grad_value, grad_text)
```

```python
import math

import jax
import jax.numpy as jnp
from jax import lax
from jax.experimental import pallas as pl
from jax.experimental.pallas import tpu as pltpu
from jax.sharding import PartitionSpec as P

HD = 128
REACH = 2
OFFSETS = (0, 1, -1, 2, -2)
MASKED_SCORE = -1e30
ROOT = HD ** (-0.5)
LOG2E = math.log2(math.e)
F32 = jnp.float32
BF16 = jnp.bfloat16


def nt(a, b):
    return lax.dot_general(a, b, (((1,), (1,)), ((), ())), preferred_element_type=F32)


def nn(a, b):
    return lax.dot_general(a, b, (((1,), (0,)), ((), ())), preferred_element_type=F32)


def tn(a, b):
    return lax.dot_general(a, b, (((0,), (0,)), ((), ())), preferred_element_type=F32)


def fold8(op, x):
    return op(x.reshape(x.shape[0] // 8, 8, x.shape[1]), axis=0)


def attention_kernel(meta, *refs):
    n = len(OFFSETS)
    qg = refs[0:2]
    kv = [refs[2 + 2 * i : 4 + 2 * i] for i in range(n)]
    text = refs[2 + 2 * n]
    outs = refs[3 + 2 * n :]
    out_q = outs[0:2]
    out_kv = [outs[2 + 2 * i : 4 + 2 * i] for i in range(n)]
    out_text = outs[2 + 2 * n]
    q_s, g_s, gt_s, s_s, p_s, top_s, sum_s, acc_s = outs[3 + 2 * n :]
    half = qg[0].shape[1]
    text_rows = text.shape[1]

    for h in range(2):
        q_s[h * half : (h + 1) * half] = qg[h][0]
        g_s[h * half : (h + 1) * half] = qg[h][1]
    gt_s[...] = g_s[...].astype(F32).T
    scale2 = ROOT * LOG2E

    row = lax.broadcasted_iota(jnp.int32, (text_rows, 1), 0)
    live = (row ^ meta[n + 1]) < meta[n]
    ts = jnp.where(live, nt(text[0], q_s[...]), MASKED_SCORE)
    ttop = jnp.max(ts, axis=0, keepdims=True)
    te = jnp.exp2((ts - ttop) * scale2)
    tp = (te * (1.0 / jnp.sum(te, axis=0, keepdims=True))).astype(BF16)
    tout = tn(text[1], tp)
    tdot = jnp.sum(tout * gt_s[...], axis=0, keepdims=True)
    out_text[1] = nn(tp, g_s[...]).astype(out_text.dtype)
    tds = (tp.astype(F32) * (nt(text[1], g_s[...]) - tdot)).astype(BF16)
    out_text[0] = (nn(tds, q_s[...]) * ROOT).astype(out_text.dtype)
    acc_s[1] = tn(text[0], tds)

    def scores(i):
        for h in range(2):
            s = nt(kv[i][h][0], q_s[...])
            s_s[i, h * half : (h + 1) * half] = s
            top = fold8(jnp.max, s)
            if i == 0 and h == 0:
                top_s[...] = top
            else:
                top_s[...] = jnp.maximum(top_s[...], top)

    def exps(i):
        top = jnp.max(top_s[...], axis=0, keepdims=True)
        for h in range(2):
            e = jnp.exp2((s_s[i, h * half : (h + 1) * half] - top) * scale2)
            s_s[i, h * half : (h + 1) * half] = e
            part = fold8(jnp.sum, e)
            if i == 0 and h == 0:
                sum_s[...] = part
            else:
                sum_s[...] += part

    def values(i):
        inverse = 1.0 / jnp.sum(sum_s[...], axis=0, keepdims=True)
        for h in range(2):
            p = (s_s[i, h * half : (h + 1) * half] * inverse).astype(BF16)
            p_s[i, h * half : (h + 1) * half] = p
            o = tn(kv[i][h][1], p)
            if i == 0 and h == 0:
                acc_s[0] = o
            else:
                acc_s[0] += o
            out_kv[i][h][1] = nn(p, g_s[...]).astype(BF16)

    def grads(i):
        dot = top_s[0:1]
        for h in range(2):
            dp = nt(kv[i][h][1], g_s[...])
            p = p_s[i, h * half : (h + 1) * half].astype(F32)
            ds = (p * (dp - dot)).astype(BF16)
            out_kv[i][h][0] = (nn(ds, q_s[...]) * ROOT).astype(BF16)
            acc_s[1] += tn(kv[i][h][0], ds)

    def each(step):
        step(0)
        for i in range(1, n):
            pl.when(meta[i] > 0)(lambda i=i: step(i))

    each(scores)
    each(exps)
    each(values)
    self_out = acc_s[0]
    top_s[0:1] = jnp.sum(self_out * gt_s[...], axis=0, keepdims=True)
    rows_out = (self_out + tout).T.astype(BF16)
    each(grads)
    for i in range(1, n):

        @pl.when(meta[i] == 0)
        def _():
            for h in range(2):
                out_kv[i][h][...] = jnp.zeros_like(out_kv[i][h])

    rows_dq = (acc_s[1] * ROOT).T.astype(BF16)
    for h in range(2):
        out_q[h][0] = rows_out[h * half : (h + 1) * half]
        out_q[h][1] = rows_dq[h * half : (h + 1) * half]


def attention(meta, qg, kv, text):
    half, width = qg[0].shape[1:]
    heads = width // HD
    rows = 2 * half
    text_rows = text.shape[1]
    n = len(OFFSETS)
    tile = pl.BlockSpec((2, half, HD), lambda h, meta: (0, 0, h))
    text_tile = pl.BlockSpec((2, text_rows, HD), lambda h, meta: (0, 0, h))
    part = jax.ShapeDtypeStruct((2, half, width), BF16)
    keys = 3 * rows + text_rows
    return pl.pallas_call(
        attention_kernel,
        grid_spec=pltpu.PrefetchScalarGridSpec(
            num_scalar_prefetch=1,
            grid=(heads,),
            in_specs=[tile] * (2 + 2 * n) + [text_tile],
            out_specs=[tile] * (2 + 2 * n) + [text_tile],
            scratch_shapes=[
                pltpu.VMEM((rows, HD), BF16),
                pltpu.VMEM((rows, HD), BF16),
                pltpu.VMEM((HD, rows), F32),
                pltpu.VMEM((n, rows, rows), F32),
                pltpu.VMEM((n, rows, rows), BF16),
                pltpu.VMEM((8, rows), F32),
                pltpu.VMEM((8, rows), F32),
                pltpu.VMEM((2, HD, rows), F32),
            ],
        ),
        out_shape=[part] * (2 + 2 * n) + [jax.ShapeDtypeStruct((2, text_rows, width), BF16)],
        compiler_params=pltpu.CompilerParams(vmem_limit_bytes=48 * 2**20),
        cost_estimate=pl.CostEstimate(
            flops=12 * heads * rows * keys * HD,
            bytes_accessed=2 * (4 + 4 * n + 2) * half * width * 2,
            transcendentals=heads * rows * keys,
        ),
        name="attention",
    )(meta, *qg, *[part for pair in kv for part in pair], text)


def place_kernel(meta, *refs):
    pieces = refs[0:4]
    outs = refs[4:]
    width = pieces[0].shape[2]
    for m in range(4):
        start = pl.multiple_of((meta[0] ^ m) * width, width)
        for i, out in enumerate(outs):
            out[:, pl.ds(start, width)] = pieces[m][i].astype(out.dtype)


def place(enc, pieces, dtypes):
    _, rows, width = pieces[0].shape
    return pl.pallas_call(
        place_kernel,
        in_specs=[pl.BlockSpec(memory_space=pltpu.SMEM)] + [pl.BlockSpec(memory_space=pltpu.VMEM)] * 4,
        out_specs=[pl.BlockSpec(memory_space=pltpu.VMEM)] * len(dtypes),
        out_shape=[jax.ShapeDtypeStruct((rows, 4 * width), d) for d in dtypes],
        compiler_params=pltpu.CompilerParams(vmem_limit_bytes=24 * 2**20),
        cost_estimate=pl.CostEstimate(flops=0, bytes_accessed=rows * width * 4 * 12, transcendentals=0),
        name="place",
    )(enc, *pieces)


def shards(qkv, grad_out, text_kv, text_len, key_tiles, key_count):
    ctx_size, enc_size = lax.axis_size("ctx"), lax.axis_size("enc")
    ctx, enc = lax.axis_index("ctx"), lax.axis_index("enc")
    width = qkv.shape[2] // enc_size
    rows = qkv.shape[1]

    def send(block, target):
        route = []
        for c in range(ctx_size):
            for e in range(enc_size):
                to = target(c, e)
                if 0 <= to[0] < ctx_size:
                    route.append((c * enc_size + e, to[0] * enc_size + to[1]))
        return lax.ppermute(block, ("ctx", "enc"), route)

    def swap(block, m):
        return send(block, lambda c, e: (c, e ^ m))

    def shift(block, d):
        return send(block, lambda c, e: (c + d, e))

    def across(block, m):
        return send(block, lambda c, e: (c ^ m, e))

    def columns(block, m):
        return lax.dynamic_slice_in_dim(block, (enc ^ m) * width, width, block.ndim - 1)

    kv_own = qkv[1:3]
    kv_in = [swap(columns(kv_own, m), m) if m else columns(kv_own, m) for m in range(4)]
    kv_halves = [jnp.concatenate(kv_in[0:2], 1), jnp.concatenate(kv_in[2:4], 1)]
    near = {0: kv_halves, 1: [None, None], -1: [None, None], 2: [None, None], -2: [None, None]}
    for h in range(2):
        for sign in (1, -1):
            near[sign][h] = shift(kv_halves[h], -sign)
        for sign in (1, -1):
            near[2 * sign][h] = shift(near[sign][h], -sign)

    def qg_columns(m):
        return jnp.stack([columns(qkv[0], m), columns(grad_out, m)])

    qg_in = [swap(qg_columns(m), m) if m else qg_columns(m) for m in range(4)]
    qg = [jnp.concatenate(qg_in[0:2], 1), jnp.concatenate(qg_in[2:4], 1)]

    text = text_kv
    for step in (1, 4, 16):
        text = jnp.concatenate([text] + [across(text, m * step) for m in (1, 2, 3)], 1)

    my_tiles = lax.dynamic_index_in_dim(key_tiles, ctx, 0, keepdims=False)
    my_count = lax.dynamic_index_in_dim(key_count, ctx, 0, keepdims=False)
    listed = jnp.arange(my_tiles.shape[0]) < my_count
    meta = jnp.stack(
        [jnp.any(listed & (my_tiles - ctx == o)).astype(jnp.int32) for o in OFFSETS]
        + [text_len[0], ctx * text_kv.shape[1]]
    ).astype(jnp.int32)

    outs = attention(meta, qg, [near[o] for o in OFFSETS], text)
    out_q = outs[0:2]
    terms = {o: outs[2 + 2 * i : 4 + 2 * i] for i, o in enumerate(OFFSETS)}
    text_terms = outs[2 + 2 * len(OFFSETS)]

    grad_halves = [None, None]
    for h in (1, 0):
        total = terms[0][h].astype(F32)
        for sign in (1, -1):
            far = shift(terms[2 * sign][h], sign)
            mid = (terms[sign][h].astype(F32) + far.astype(F32)).astype(BF16)
            total = total + shift(mid, sign).astype(F32)
        grad_halves[h] = total.astype(BF16)

    def back(halves):
        pieces = []
        for m in range(4):
            piece = halves[m // 2][:, (m % 2) * rows : (m % 2 + 1) * rows]
            pieces.append(swap(piece, m) if m else piece)
        return pieces

    meta_enc = enc.astype(jnp.int32).reshape(1)
    attn_out, grad_q = place(meta_enc, back(out_q), (BF16, F32))
    grad_k, grad_v = place(meta_enc, back(grad_halves), (F32, F32))

    grad_text = text_terms
    for step in (16, 4, 1):
        size = grad_text.shape[1] // 4
        total = grad_text[:, 0:size].astype(F32)
        for m in (1, 2, 3):
            total = total + across(grad_text[:, m * size : (m + 1) * size], m * step).astype(F32)
        grad_text = total if step == 1 else total.astype(BF16)
    return (attn_out, grad_q, grad_k, grad_v, grad_text)


def solution(mesh):
    in_specs = (
        P(None, ("ctx", "enc"), None),
        P(("ctx", "enc"), None),
        P(None, "ctx", "enc"),
        P(),
        P(),
        P(),
    )
    out_specs = (
        P(("ctx", "enc"), None),
        P(("ctx", "enc"), None),
        P(("ctx", "enc"), None),
        P(("ctx", "enc"), None),
        P(None, "ctx", "enc"),
    )
    return jax.shard_map(shards, mesh=mesh, in_specs=in_specs, out_specs=out_specs, check_vma=False)
```

```python
import math

import jax
import jax.numpy as jnp
from jax import lax
from jax.experimental import pallas as pl
from jax.experimental.pallas import tpu as pltpu
from jax.sharding import Mesh, PartitionSpec as P

HD = 128
SOURCES = 6
MASKED_SCORE = -1e30
ROOT = HD ** (-0.5)
LOG2E = math.log2(math.e)
F32 = jnp.float32
BF16 = jnp.bfloat16


def nt(a, b):
    return lax.dot_general(a, b, (((1,), (1,)), ((), ())), preferred_element_type=F32)


def nn(a, b):
    return lax.dot_general(a, b, (((1,), (0,)), ((), ())), preferred_element_type=F32)


def tn(a, b):
    return lax.dot_general(a, b, (((0,), (0,)), ((), ())), preferred_element_type=F32)


def fold8(op, x):
    return op(x.reshape(x.shape[0] // 8, 8, x.shape[1]), axis=0)


def load_rows(qg, q_s, g_s, gt_s):
    half = qg[0].shape[1]
    for h in range(2):
        q_s[h * half : (h + 1) * half] = qg[h][0]
        g_s[h * half : (h + 1) * half] = qg[h][1]
    gt_s[...] = g_s[...].astype(F32).T


def text_kernel(text_len, qg0, qg1, text, out_terms, out_rows, out_dq, q_s, g_s, gt_s):
    load_rows((qg0, qg1), q_s, g_s, gt_s)
    parts, _, part_rows, _ = text.shape
    keys = text[:, 0].reshape(parts * part_rows, HD)
    values = text[:, 1].reshape(parts * part_rows, HD)
    row = lax.broadcasted_iota(jnp.int32, (parts * part_rows, 1), 0)
    s = jnp.where(row < text_len[0], nt(keys, q_s[...]), MASKED_SCORE)
    e = jnp.exp2((s - jnp.max(s, axis=0, keepdims=True)) * (ROOT * LOG2E))
    p = (e * (1.0 / jnp.sum(e, axis=0, keepdims=True))).astype(BF16)
    rows = tn(values, p)
    dot = jnp.sum(rows * gt_s[...], axis=0, keepdims=True)
    ds = (p.astype(F32) * (nt(values, g_s[...]) - dot)).astype(BF16)
    out_rows[...] = rows
    out_dq[...] = tn(keys, ds)
    out_terms[:, 0] = (nn(ds, q_s[...]) * ROOT).astype(BF16).reshape(parts, part_rows, HD)
    out_terms[:, 1] = nn(p, g_s[...]).astype(BF16).reshape(parts, part_rows, HD)


def text_attention(text_len, qg, text):
    half, width = qg[0].shape[1:]
    heads = width // HD
    rows = 2 * half
    tile = pl.BlockSpec((2, half, HD), lambda h, n: (0, 0, h))
    text_tile = pl.BlockSpec((*text.shape[:3], HD), lambda h, n: (0, 0, 0, h))
    turned = pl.BlockSpec((HD, rows), lambda h, n: (h, 0))
    text_rows = text.shape[0] * text.shape[2]
    return pl.pallas_call(
        text_kernel,
        grid_spec=pltpu.PrefetchScalarGridSpec(
            num_scalar_prefetch=1,
            grid=(heads,),
            in_specs=[tile, tile, text_tile],
            out_specs=[text_tile, turned, turned],
            scratch_shapes=[
                pltpu.VMEM((rows, HD), BF16),
                pltpu.VMEM((rows, HD), BF16),
                pltpu.VMEM((HD, rows), F32),
            ],
        ),
        out_shape=[
            jax.ShapeDtypeStruct(text.shape, BF16),
            jax.ShapeDtypeStruct((width, rows), F32),
            jax.ShapeDtypeStruct((width, rows), F32),
        ],
        compiler_params=pltpu.CompilerParams(vmem_limit_bytes=32 * 2**20),
        cost_estimate=pl.CostEstimate(
            flops=12 * heads * rows * text_rows * HD,
            bytes_accessed=16 * half * width,
            transcendentals=heads * rows * text_rows,
        ),
        name="text_attention",
    )(text_len, *qg, text)


def attention_kernel(meta, *refs):
    n = SOURCES
    qg = refs[0:2]
    kv = [refs[2 + 2 * i : 4 + 2 * i] for i in range(n)]
    text_rows, text_dq = refs[2 + 2 * n : 4 + 2 * n]
    outs = refs[4 + 2 * n :]
    out_q = outs[0:2]
    out_kv = [outs[2 + 2 * i : 4 + 2 * i] for i in range(n)]
    q_s, g_s, gt_s, s_s, p_s, top_s, sum_s, acc_s = outs[2 + 2 * n :]
    half = qg[0].shape[1]
    scale2 = ROOT * LOG2E
    load_rows(qg, q_s, g_s, gt_s)
    acc_s[1] = text_dq[...]

    def scores(i):
        for h in range(2):
            s = nt(kv[i][h][0], q_s[...])
            s_s[i, h * half : (h + 1) * half] = s
            top = fold8(jnp.max, s)
            if i == 0 and h == 0:
                top_s[...] = top
            else:
                top_s[...] = jnp.maximum(top_s[...], top)

    def exps(i):
        top = jnp.max(top_s[...], axis=0, keepdims=True)
        for h in range(2):
            e = jnp.exp2((s_s[i, h * half : (h + 1) * half] - top) * scale2)
            s_s[i, h * half : (h + 1) * half] = e
            part = fold8(jnp.sum, e)
            if i == 0 and h == 0:
                sum_s[...] = part
            else:
                sum_s[...] += part

    def values(i):
        inverse = 1.0 / jnp.sum(sum_s[...], axis=0, keepdims=True)
        for h in range(2):
            p = (s_s[i, h * half : (h + 1) * half] * inverse).astype(BF16)
            p_s[i, h * half : (h + 1) * half] = p
            o = tn(kv[i][h][1], p)
            if i == 0 and h == 0:
                acc_s[0] = o
            else:
                acc_s[0] += o
            out_kv[i][h][1] = nn(p, g_s[...]).astype(BF16)

    def grads(i):
        dot = top_s[0:1]
        for h in range(2):
            dp = nt(kv[i][h][1], g_s[...])
            p = p_s[i, h * half : (h + 1) * half].astype(F32)
            ds = (p * (dp - dot)).astype(BF16)
            out_kv[i][h][0] = (nn(ds, q_s[...]) * ROOT).astype(BF16)
            acc_s[1] += tn(kv[i][h][0], ds)

    def each(step):
        step(0)
        for i in range(1, n):
            pl.when(meta[i] > 0)(lambda i=i: step(i))

    each(scores)
    each(exps)
    each(values)
    self_out = acc_s[0]
    top_s[0:1] = jnp.sum(self_out * gt_s[...], axis=0, keepdims=True)
    rows_out = (self_out + text_rows[...]).T.astype(BF16)
    each(grads)
    for i in range(1, n):

        @pl.when(meta[i] == 0)
        def _():
            for h in range(2):
                out_kv[i][h][...] = jnp.zeros_like(out_kv[i][h])

    rows_dq = (acc_s[1] * ROOT).T.astype(BF16)
    for h in range(2):
        out_q[h][0] = rows_out[h * half : (h + 1) * half]
        out_q[h][1] = rows_dq[h * half : (h + 1) * half]


def attention(meta, qg, kv, text_rows, text_dq):
    half, width = qg[0].shape[1:]
    heads = width // HD
    rows = 2 * half
    n = SOURCES
    tile = pl.BlockSpec((2, half, HD), lambda h, meta: (0, 0, h))
    turned = pl.BlockSpec((HD, rows), lambda h, meta: (h, 0))
    part = jax.ShapeDtypeStruct((2, half, width), BF16)
    keys = 3 * rows
    return pl.pallas_call(
        attention_kernel,
        grid_spec=pltpu.PrefetchScalarGridSpec(
            num_scalar_prefetch=1,
            grid=(heads,),
            in_specs=[tile] * (2 + 2 * n) + [turned, turned],
            out_specs=[tile] * (2 + 2 * n),
            scratch_shapes=[
                pltpu.VMEM((rows, HD), BF16),
                pltpu.VMEM((rows, HD), BF16),
                pltpu.VMEM((HD, rows), F32),
                pltpu.VMEM((n, rows, rows), F32),
                pltpu.VMEM((n, rows, rows), BF16),
                pltpu.VMEM((8, rows), F32),
                pltpu.VMEM((8, rows), F32),
                pltpu.VMEM((2, HD, rows), F32),
            ],
        ),
        out_shape=[part] * (2 + 2 * n),
        compiler_params=pltpu.CompilerParams(vmem_limit_bytes=48 * 2**20),
        cost_estimate=pl.CostEstimate(
            flops=12 * heads * rows * keys * HD,
            bytes_accessed=2 * (4 + 4 * n) * half * width * 2,
            transcendentals=heads * rows * keys,
        ),
        name="attention",
    )(meta, *qg, *[part for pair in kv for part in pair], text_rows, text_dq)


def place_kernel(meta, *refs):
    pieces = refs[0:4]
    outs = refs[4:]
    width = pieces[0].shape[2]
    for m in range(4):
        start = pl.multiple_of((meta[0] ^ m) * width, width)
        for i, out in enumerate(outs):
            out[:, pl.ds(start, width)] = pieces[m][i].astype(out.dtype)


def place(enc, pieces, dtypes):
    _, rows, width = pieces[0].shape
    return pl.pallas_call(
        place_kernel,
        in_specs=[pl.BlockSpec(memory_space=pltpu.SMEM)] + [pl.BlockSpec(memory_space=pltpu.VMEM)] * 4,
        out_specs=[pl.BlockSpec(memory_space=pltpu.VMEM)] * len(dtypes),
        out_shape=[jax.ShapeDtypeStruct((rows, 4 * width), d) for d in dtypes],
        compiler_params=pltpu.CompilerParams(vmem_limit_bytes=24 * 2**20),
        cost_estimate=pl.CostEstimate(flops=0, bytes_accessed=rows * width * 4 * 12, transcendentals=0),
        name="place",
    )(enc, *pieces)


CTX = ("y", "z_lo", "x")
ENC = ("z_hi", "core")
SIZES = {"y": 4, "z_lo": 4, "x": 4, "z_hi": 2, "core": 2}


def shards(qkv, grad_out, text_kv, text_len, key_tiles, key_count):
    ctx_size, enc_size = lax.axis_size(CTX), lax.axis_size(ENC)
    ctx, enc = lax.axis_index(CTX), lax.axis_index(ENC)
    width = qkv.shape[2] // enc_size
    rows = qkv.shape[1]
    plane = ("z_lo", "x")
    row_len = lax.axis_size("x")
    lane = lax.axis_index("x")
    even = lane % 2 == 0

    def send(block, target):
        route = []
        for c in range(ctx_size):
            for e in range(enc_size):
                to = target(c, e)
                if 0 <= to[0] < ctx_size:
                    route.append((c * enc_size + e, to[0] * enc_size + to[1]))
        return lax.ppermute(block, CTX + ENC, route)

    def swap(block, m):
        return send(block, lambda c, e: (c, e ^ m))

    def rotate(block, d):
        return send(block, lambda c, e: (c - c % row_len + (c + d) % row_len, e))

    def pair(block):
        return send(block, lambda c, e: (c ^ 1, e))

    def next_row(block, sign):
        return send(block, lambda c, e: (c + sign * (row_len if c % row_len < 2 else -row_len), e))

    def columns(block, m):
        return lax.dynamic_slice_in_dim(block, (enc ^ m) * width, width, block.ndim - 1)

    def tie(blocks, done):
        return lax.optimization_barrier((blocks, done))

    text = text_kv.reshape(1, -1, width)
    text = jnp.broadcast_to(text, (lax.axis_size(plane), *text.shape[1:]))
    text = lax.all_to_all(text, plane, split_axis=0, concat_axis=0, tiled=True)
    text = text.reshape(-1, *text_kv.shape).transpose(1, 0, 2, 3).reshape(2, -1, width)

    kv_own = [columns(qkv[1:3], m) for m in range(4)]
    kv_in = [swap(kv_own[m], m) if m else kv_own[m] for m in range(4)]
    own = [jnp.concatenate(kv_in[0:2], 1), None]
    left, right, far, across, paired = ([None, None] for _ in range(5))
    qg_in = [None] * 4

    def qg_columns(q, g, m):
        return jnp.stack([columns(q, m), columns(g, m)])

    left[0], right[0] = rotate(own[0], 1), rotate(own[0], -1)
    across[0] = next_row(jnp.where(even, left[0], right[0]), 1)
    far[0] = rotate(left[0], 1)
    q_g = (qkv[0], grad_out)
    (kv_in[2:4], q_g), (left[0], right[0], far[0], text) = tie(
        (kv_in[2:4], q_g), (left[0], right[0], far[0], text)
    )
    text = lax.all_gather(text, "y", axis=0)

    own[1] = jnp.concatenate(kv_in[2:4], 1)
    qg_in[3] = swap(qg_columns(*q_g, 3), 3)
    qg_in[1] = swap(qg_columns(*q_g, 1), 1)
    left[1], right[1] = rotate(own[1], 1), rotate(own[1], -1)
    (left[1], right[1], across[0]), (qg_in[3], q_g) = tie((left[1], right[1], across[0]), (qg_in[3], q_g))

    across[1] = next_row(jnp.where(even, left[1], right[1]), 1)
    qg_in[2] = swap(qg_columns(*q_g, 2), 2)
    far[1] = rotate(right[1], -1)
    paired[0] = pair(across[0])
    across[1], (qg_in[2], far[1], paired[0], text) = tie(across[1], (qg_in[2], far[1], paired[0], text))

    paired[1] = pair(across[1])
    qg_in[0] = qg_columns(*q_g, 0)
    qg = [jnp.concatenate(qg_in[0:2], 1), jnp.concatenate(qg_in[2:4], 1)]
    grad_text, text_rows, text_dq = text_attention(text_len, qg, text)
    paired[1], (grad_text, text_rows, text_dq) = tie(paired[1], (grad_text, text_rows, text_dq))
    grad_text = lax.psum_scatter(grad_text, "y", scatter_dimension=0)

    my_tiles = lax.dynamic_index_in_dim(key_tiles, ctx, 0, keepdims=False)
    my_count = lax.dynamic_index_in_dim(key_count, ctx, 0, keepdims=False)
    listed = jnp.arange(my_tiles.shape[0]) < my_count
    row = ctx - lane
    outer = (lane == 0) | (lane == row_len - 1)
    side = jnp.where(lane < 2, -1, 1)
    sources = jnp.stack(
        [
            ctx,
            row + (lane + row_len - 1) % row_len,
            row + (lane + 1) % row_len,
            row + (lane + 2) % row_len,
            ctx + 2 * side,
            jnp.where(outer, ctx + side, -1),
        ]
    )
    used = (my_tiles[None, :] == sources[:, None]) & listed[None, :]
    meta = jnp.sum(used, axis=1).astype(jnp.int32)

    outs = attention(meta, qg, [own, left, right, far, paired, across], text_rows, text_dq)
    out_q = outs[0:2]
    terms = [list(outs[2 + 2 * i : 4 + 2 * i]) for i in range(SOURCES)]
    t_own, t_left, t_right, t_far, t_paired, t_across = terms

    def piece(halves, m):
        return halves[m // 2][:, (m % 2) * rows : (m % 2 + 1) * rows]

    def add(*blocks):
        return sum(b.astype(F32) for b in blocks).astype(BF16)

    back_q = [piece(out_q, m) for m in range(4)]
    met, relayed, crossed, to_right, to_left, grad_halves = ([None, None] for _ in range(6))

    back_q[1], back_q[2] = swap(back_q[1], 1), swap(back_q[2], 2)
    met[1] = pair(t_paired[1])
    met[1], (back_q[2], back_q[3], t_far[1], t_paired[0], grad_text) = tie(
        met[1], (back_q[2], back_q[3], t_far[1], t_paired[0], grad_text)
    )
    grad_text = grad_text.reshape(2, -1, text_kv.shape[1], width).transpose(1, 0, 2, 3)
    grad_text = grad_text.reshape(-1, 2 * text_kv.shape[1], width)
    grad_text = lax.all_to_all(grad_text, plane, split_axis=0, concat_axis=0, tiled=True)

    crossed[1] = next_row(add(t_across[1], met[1]), -1)
    back_q[3] = swap(back_q[3], 3)
    relayed[1] = rotate(t_far[1], 1)
    met[0] = pair(t_paired[0])
    (crossed[1], relayed[1]), (met[0], back_q[3], t_far[0], grad_text) = tie(
        (crossed[1], relayed[1]), (met[0], back_q[3], t_far[0], grad_text)
    )

    def totals(h):
        none = jnp.zeros_like(crossed[h])
        to_right = add(t_right[h], jnp.where(even, none, crossed[h]), *([relayed[h]] if h else []))
        to_left = add(t_left[h], jnp.where(even, crossed[h], none), *([] if h else [relayed[h]]))
        return rotate(to_right, 1), rotate(to_left, -1)

    last = totals(1)
    crossed[0] = next_row(add(t_across[0], met[0]), -1)
    relayed[0] = rotate(t_far[0], -1)
    last, (crossed[0], relayed[0]) = tie(last, (crossed[0], relayed[0]))
    grad_halves[1] = add(t_own[1], *last)
    grad_halves[0] = add(t_own[0], *totals(0))
    back_kv = [piece(grad_halves, m) for m in range(4)]
    back_kv[1:4] = [swap(back_kv[m], m) for m in (1, 2, 3)]

    grad_text = jnp.sum(grad_text.astype(F32), axis=0).reshape(text_kv.shape)

    meta_enc = enc.astype(jnp.int32).reshape(1)
    attn_out, grad_q = place(meta_enc, back_q, (BF16, F32))
    grad_k, grad_v = place(meta_enc, back_kv, (F32, F32))
    return (attn_out, grad_q, grad_k, grad_v, grad_text)


def solution(mesh):
    fine = Mesh(mesh.devices.reshape(tuple(SIZES.values())), tuple(SIZES))
    tokens = P(CTX + ENC, None)
    in_specs = (P(None, CTX + ENC, None), tokens, P(None, CTX, ENC), P(), P(), P())
    out_specs = (tokens, tokens, tokens, tokens, P(None, CTX, ENC))
    return jax.shard_map(shards, mesh=fine, in_specs=in_specs, out_specs=out_specs, check_vma=False)
```

```python
import math

import jax
import jax.numpy as jnp
from jax import lax
from jax.experimental import pallas as pl
from jax.experimental.pallas import tpu as pltpu
from jax.sharding import Mesh, PartitionSpec as P

HD = 128
SOURCES = 6
MASKED_SCORE = -1e30
ROOT = HD ** (-0.5)
LOG2E = math.log2(math.e)
F32 = jnp.float32
BF16 = jnp.bfloat16


def nt(a, b):
    return lax.dot_general(a, b, (((1,), (1,)), ((), ())), preferred_element_type=F32)


def nn(a, b):
    return lax.dot_general(a, b, (((1,), (0,)), ((), ())), preferred_element_type=F32)


def tn(a, b):
    return lax.dot_general(a, b, (((0,), (0,)), ((), ())), preferred_element_type=F32)


def fold8(op, x):
    return op(x.reshape(x.shape[0] // 8, 8, x.shape[1]), axis=0)


def load_rows(qg, q_s, g_s, gt_s):
    half = qg[0].shape[1]
    for h in range(2):
        q_s[h * half : (h + 1) * half] = qg[h][0]
        g_s[h * half : (h + 1) * half] = qg[h][1]
    gt_s[...] = g_s[...].astype(F32).T


def text_kernel(text_len, qg0, qg1, text, out_terms, out_rows, out_dq, q_s, g_s, gt_s):
    load_rows((qg0, qg1), q_s, g_s, gt_s)
    parts, _, part_rows, _ = text.shape
    keys = text[:, 0].reshape(parts * part_rows, HD)
    values = text[:, 1].reshape(parts * part_rows, HD)
    row = lax.broadcasted_iota(jnp.int32, (parts * part_rows, 1), 0)
    s = jnp.where(row < text_len[0], nt(keys, q_s[...]), MASKED_SCORE)
    e = jnp.exp2((s - jnp.max(s, axis=0, keepdims=True)) * (ROOT * LOG2E))
    p = (e * (1.0 / jnp.sum(e, axis=0, keepdims=True))).astype(BF16)
    rows = tn(values, p)
    dot = jnp.sum(rows * gt_s[...], axis=0, keepdims=True)
    ds = (p.astype(F32) * (nt(values, g_s[...]) - dot)).astype(BF16)
    out_rows[...] = rows
    out_dq[...] = tn(keys, ds)
    out_terms[:, 0] = (nn(ds, q_s[...]) * ROOT).astype(BF16).reshape(parts, part_rows, HD)
    out_terms[:, 1] = nn(p, g_s[...]).astype(BF16).reshape(parts, part_rows, HD)


def text_attention(text_len, qg, text):
    half, width = qg[0].shape[1:]
    heads = width // HD
    rows = 2 * half
    tile = pl.BlockSpec((2, half, HD), lambda h, n: (0, 0, h))
    text_tile = pl.BlockSpec((*text.shape[:3], HD), lambda h, n: (0, 0, 0, h))
    turned = pl.BlockSpec((HD, rows), lambda h, n: (h, 0))
    text_rows = text.shape[0] * text.shape[2]
    return pl.pallas_call(
        text_kernel,
        grid_spec=pltpu.PrefetchScalarGridSpec(
            num_scalar_prefetch=1,
            grid=(heads,),
            in_specs=[tile, tile, text_tile],
            out_specs=[text_tile, turned, turned],
            scratch_shapes=[
                pltpu.VMEM((rows, HD), BF16),
                pltpu.VMEM((rows, HD), BF16),
                pltpu.VMEM((HD, rows), F32),
            ],
        ),
        out_shape=[
            jax.ShapeDtypeStruct(text.shape, BF16),
            jax.ShapeDtypeStruct((width, rows), F32),
            jax.ShapeDtypeStruct((width, rows), F32),
        ],
        compiler_params=pltpu.CompilerParams(vmem_limit_bytes=32 * 2**20),
        cost_estimate=pl.CostEstimate(
            flops=12 * heads * rows * text_rows * HD,
            bytes_accessed=16 * half * width,
            transcendentals=heads * rows * text_rows,
        ),
        name="text_attention",
    )(text_len, *qg, text)


def attention_kernel(meta, *refs):
    n = SOURCES
    qg = refs[0:2]
    kv = [refs[2 + 2 * i : 4 + 2 * i] for i in range(n)]
    text_rows, text_dq = refs[2 + 2 * n : 4 + 2 * n]
    outs = refs[4 + 2 * n :]
    out_q = outs[0:2]
    out_kv = [outs[2 + 2 * i : 4 + 2 * i] for i in range(n)]
    q_s, g_s, gt_s, s_s, p_s, top_s, sum_s, acc_s = outs[2 + 2 * n :]
    half = qg[0].shape[1]
    scale2 = ROOT * LOG2E
    load_rows(qg, q_s, g_s, gt_s)
    acc_s[1] = text_dq[...]

    def scores(i):
        for h in range(2):
            s = nt(kv[i][h][0], q_s[...])
            s_s[i, h * half : (h + 1) * half] = s
            top = fold8(jnp.max, s)
            if i == 0 and h == 0:
                top_s[...] = top
            else:
                top_s[...] = jnp.maximum(top_s[...], top)

    def exps(i):
        top = jnp.max(top_s[...], axis=0, keepdims=True)
        for h in range(2):
            e = jnp.exp2((s_s[i, h * half : (h + 1) * half] - top) * scale2)
            s_s[i, h * half : (h + 1) * half] = e
            part = fold8(jnp.sum, e)
            if i == 0 and h == 0:
                sum_s[...] = part
            else:
                sum_s[...] += part

    def values(i):
        inverse = 1.0 / jnp.sum(sum_s[...], axis=0, keepdims=True)
        for h in range(2):
            p = (s_s[i, h * half : (h + 1) * half] * inverse).astype(BF16)
            p_s[i, h * half : (h + 1) * half] = p
            o = tn(kv[i][h][1], p)
            if i == 0 and h == 0:
                acc_s[0] = o
            else:
                acc_s[0] += o
            out_kv[i][h][1] = nn(p, g_s[...]).astype(BF16)

    def grads(i):
        dot = top_s[0:1]
        for h in range(2):
            dp = nt(kv[i][h][1], g_s[...])
            p = p_s[i, h * half : (h + 1) * half].astype(F32)
            ds = (p * (dp - dot)).astype(BF16)
            out_kv[i][h][0] = (nn(ds, q_s[...]) * ROOT).astype(BF16)
            acc_s[1] += tn(kv[i][h][0], ds)

    def each(step):
        step(0)
        for i in range(1, n):
            pl.when(meta[i] > 0)(lambda i=i: step(i))

    each(scores)
    each(exps)
    each(values)
    self_out = acc_s[0]
    top_s[0:1] = jnp.sum(self_out * gt_s[...], axis=0, keepdims=True)
    rows_out = (self_out + text_rows[...]).T.astype(BF16)
    each(grads)
    for i in range(1, n):

        @pl.when(meta[i] == 0)
        def _():
            for h in range(2):
                out_kv[i][h][...] = jnp.zeros_like(out_kv[i][h])

    rows_dq = (acc_s[1] * ROOT).T.astype(BF16)
    for h in range(2):
        out_q[h][0] = rows_out[h * half : (h + 1) * half]
        out_q[h][1] = rows_dq[h * half : (h + 1) * half]


def attention(meta, qg, kv, text_rows, text_dq):
    half, width = qg[0].shape[1:]
    heads = width // HD
    rows = 2 * half
    n = SOURCES
    tile = pl.BlockSpec((2, half, HD), lambda h, meta: (0, 0, h))
    turned = pl.BlockSpec((HD, rows), lambda h, meta: (h, 0))
    part = jax.ShapeDtypeStruct((2, half, width), BF16)
    keys = 3 * rows
    return pl.pallas_call(
        attention_kernel,
        grid_spec=pltpu.PrefetchScalarGridSpec(
            num_scalar_prefetch=1,
            grid=(heads,),
            in_specs=[tile] * (2 + 2 * n) + [turned, turned],
            out_specs=[tile] * (2 + 2 * n),
            scratch_shapes=[
                pltpu.VMEM((rows, HD), BF16),
                pltpu.VMEM((rows, HD), BF16),
                pltpu.VMEM((HD, rows), F32),
                pltpu.VMEM((n, rows, rows), F32),
                pltpu.VMEM((n, rows, rows), BF16),
                pltpu.VMEM((8, rows), F32),
                pltpu.VMEM((8, rows), F32),
                pltpu.VMEM((2, HD, rows), F32),
            ],
        ),
        out_shape=[part] * (2 + 2 * n),
        compiler_params=pltpu.CompilerParams(vmem_limit_bytes=48 * 2**20),
        cost_estimate=pl.CostEstimate(
            flops=12 * heads * rows * keys * HD,
            bytes_accessed=2 * (4 + 4 * n) * half * width * 2,
            transcendentals=heads * rows * keys,
        ),
        name="attention",
    )(meta, *qg, *[part for pair in kv for part in pair], text_rows, text_dq)


def place_kernel(meta, *refs):
    pieces = refs[0:4]
    outs = refs[4:]
    width = pieces[0].shape[2]
    for m in range(4):
        start = pl.multiple_of((meta[0] ^ m) * width, width)
        for i, out in enumerate(outs):
            out[:, pl.ds(start, width)] = pieces[m][i].astype(out.dtype)


def place(enc, pieces, dtypes):
    _, rows, width = pieces[0].shape
    return pl.pallas_call(
        place_kernel,
        in_specs=[pl.BlockSpec(memory_space=pltpu.SMEM)] + [pl.BlockSpec(memory_space=pltpu.VMEM)] * 4,
        out_specs=[pl.BlockSpec(memory_space=pltpu.VMEM)] * len(dtypes),
        out_shape=[jax.ShapeDtypeStruct((rows, 4 * width), d) for d in dtypes],
        compiler_params=pltpu.CompilerParams(vmem_limit_bytes=24 * 2**20),
        cost_estimate=pl.CostEstimate(flops=0, bytes_accessed=rows * width * 4 * 12, transcendentals=0),
        name="place",
    )(enc, *pieces)


CTX = ("y", "z_lo", "x")
ENC = ("z_hi", "core")
SIZES = {"y": 4, "z_lo": 4, "x": 4, "z_hi": 2, "core": 2}


def shards(qkv, grad_out, text_kv, text_len, key_tiles, key_count):
    ctx_size, enc_size = lax.axis_size(CTX), lax.axis_size(ENC)
    ctx, enc = lax.axis_index(CTX), lax.axis_index(ENC)
    width = qkv.shape[2] // enc_size
    rows = qkv.shape[1]
    plane = ("z_lo", "x")
    row_len = lax.axis_size("x")
    lane = lax.axis_index("x")
    even = lane % 2 == 0

    def send(block, target):
        route = []
        for c in range(ctx_size):
            for e in range(enc_size):
                to = target(c, e)
                if 0 <= to[0] < ctx_size:
                    route.append((c * enc_size + e, to[0] * enc_size + to[1]))
        return lax.ppermute(block, CTX + ENC, route)

    def swap(block, m):
        return send(block, lambda c, e: (c, e ^ m))

    def rotate(block, d):
        return send(block, lambda c, e: (c - c % row_len + (c + d) % row_len, e))

    def pair(block):
        return send(block, lambda c, e: (c ^ 1, e))

    def next_row(block, sign):
        return send(block, lambda c, e: (c + sign * (row_len if c % row_len < 2 else -row_len), e))

    def columns(block, m):
        return lax.dynamic_slice_in_dim(block, (enc ^ m) * width, width, block.ndim - 1)

    def tie(blocks, done):
        return lax.optimization_barrier((blocks, done))

    text = text_kv.reshape(1, -1, width)
    text = jnp.broadcast_to(text, (lax.axis_size(plane), *text.shape[1:]))
    text = lax.all_to_all(text, plane, split_axis=0, concat_axis=0, tiled=True)
    text = text.reshape(-1, *text_kv.shape).transpose(1, 0, 2, 3).reshape(2, -1, width)

    kv_own = [columns(qkv[1:3], m) for m in range(4)]
    kv_in = [swap(kv_own[m], m) if m else kv_own[m] for m in range(4)]
    own = [jnp.concatenate(kv_in[0:2], 1), None]
    left, right, far, across, paired = ([None, None] for _ in range(5))
    qg_in = [None] * 4

    def qg_columns(q, g, m):
        return jnp.stack([columns(q, m), columns(g, m)])

    left[0], right[0] = rotate(own[0], 1), rotate(own[0], -1)
    across[0] = next_row(jnp.where(even, left[0], right[0]), 1)
    far[0] = rotate(left[0], 1)
    q_g = (qkv[0], grad_out)
    (kv_in[2:4], q_g), (left[0], right[0], far[0], text) = tie(
        (kv_in[2:4], q_g), (left[0], right[0], far[0], text)
    )
    text = lax.all_gather(text, "y", axis=0)

    own[1] = jnp.concatenate(kv_in[2:4], 1)
    qg_in[3] = swap(qg_columns(*q_g, 3), 3)
    qg_in[1] = swap(qg_columns(*q_g, 1), 1)
    left[1], right[1] = rotate(own[1], 1), rotate(own[1], -1)
    (left[1], right[1], across[0]), (qg_in[3], q_g) = tie((left[1], right[1], across[0]), (qg_in[3], q_g))

    across[1] = next_row(jnp.where(even, left[1], right[1]), 1)
    qg_in[2] = swap(qg_columns(*q_g, 2), 2)
    far[1] = rotate(right[1], -1)
    paired[0] = pair(across[0])
    across[1], (qg_in[2], far[1], paired[0], text) = tie(across[1], (qg_in[2], far[1], paired[0], text))

    paired[1] = pair(across[1])
    qg_in[0] = qg_columns(*q_g, 0)
    qg = [jnp.concatenate(qg_in[0:2], 1), jnp.concatenate(qg_in[2:4], 1)]
    grad_text, text_rows, text_dq = text_attention(text_len, qg, text)
    paired[1], (grad_text, text_rows, text_dq) = tie(paired[1], (grad_text, text_rows, text_dq))
    grad_text = lax.psum_scatter(grad_text, "y", scatter_dimension=0)

    my_tiles = lax.dynamic_index_in_dim(key_tiles, ctx, 0, keepdims=False)
    my_count = lax.dynamic_index_in_dim(key_count, ctx, 0, keepdims=False)
    listed = jnp.arange(my_tiles.shape[0]) < my_count
    row = ctx - lane
    outer = (lane == 0) | (lane == row_len - 1)
    side = jnp.where(lane < 2, -1, 1)
    sources = jnp.stack(
        [
            ctx,
            row + (lane + row_len - 1) % row_len,
            row + (lane + 1) % row_len,
            row + (lane + 2) % row_len,
            ctx + 2 * side,
            jnp.where(outer, ctx + side, -1),
        ]
    )
    used = (my_tiles[None, :] == sources[:, None]) & listed[None, :]
    meta = jnp.sum(used, axis=1).astype(jnp.int32)

    outs = attention(meta, qg, [own, left, right, far, paired, across], text_rows, text_dq)
    out_q = outs[0:2]
    terms = [list(outs[2 + 2 * i : 4 + 2 * i]) for i in range(SOURCES)]
    t_own, t_left, t_right, t_far, t_paired, t_across = terms

    def piece(halves, m):
        return halves[m // 2][:, (m % 2) * rows : (m % 2 + 1) * rows]

    def add(*blocks):
        return sum(b.astype(F32) for b in blocks).astype(BF16)

    back_q = [piece(out_q, m) for m in range(4)]
    met, relayed, crossed, to_right, to_left, grad_halves = ([None, None] for _ in range(6))

    back_q[1], back_q[2] = swap(back_q[1], 1), swap(back_q[2], 2)
    met[1] = pair(t_paired[1])
    met[1], (back_q[2], back_q[3], t_far[1], t_paired[0], grad_text) = tie(
        met[1], (back_q[2], back_q[3], t_far[1], t_paired[0], grad_text)
    )
    grad_text = grad_text.reshape(2, -1, text_kv.shape[1], width).transpose(1, 0, 2, 3)
    grad_text = grad_text.reshape(-1, 2 * text_kv.shape[1], width)
    grad_text = lax.all_to_all(grad_text, plane, split_axis=0, concat_axis=0, tiled=True)

    crossed[1] = next_row(add(t_across[1], met[1]), -1)
    back_q[3] = swap(back_q[3], 3)
    relayed[1] = rotate(t_far[1], 1)
    met[0] = pair(t_paired[0])
    (crossed[1], relayed[1]), (met[0], back_q[3], t_far[0]) = tie(
        (crossed[1], relayed[1]), (met[0], back_q[3], t_far[0])
    )

    def totals(h):
        none = jnp.zeros_like(crossed[h])
        to_right = add(t_right[h], jnp.where(even, none, crossed[h]), *([relayed[h]] if h else []))
        to_left = add(t_left[h], jnp.where(even, crossed[h], none), *([] if h else [relayed[h]]))
        return rotate(to_right, 1), rotate(to_left, -1)

    last = totals(1)
    crossed[0] = next_row(add(t_across[0], met[0]), -1)
    relayed[0] = rotate(t_far[0], -1)
    last, (crossed[0], relayed[0], grad_text) = tie(last, (crossed[0], relayed[0], grad_text))
    grad_halves[1] = add(t_own[1], *last)
    grad_halves[0] = add(t_own[0], *totals(0))
    back_kv = [piece(grad_halves, m) for m in range(4)]
    back_kv[1:4] = [swap(back_kv[m], m) for m in (1, 2, 3)]

    grad_text = jnp.sum(grad_text.astype(F32), axis=0).reshape(text_kv.shape)

    meta_enc = enc.astype(jnp.int32).reshape(1)
    attn_out, grad_q = place(meta_enc, back_q, (BF16, F32))
    grad_k, grad_v = place(meta_enc, back_kv, (F32, F32))
    return (attn_out, grad_q, grad_k, grad_v, grad_text)


def solution(mesh):
    fine = Mesh(mesh.devices.reshape(tuple(SIZES.values())), tuple(SIZES))
    tokens = P(CTX + ENC, None)
    in_specs = (P(None, CTX + ENC, None), tokens, P(None, CTX, ENC), P(), P(), P())
    out_specs = (tokens, tokens, tokens, tokens, P(None, CTX, ENC))
    return jax.shard_map(shards, mesh=fine, in_specs=in_specs, out_specs=out_specs, check_vma=False)
```
